32 devices in a mesh: region: 4 (over y, x), blk: 8 (over z, core).
Axes of the slice: x: 2, y: 2, z: 4, core: 2. Of those that a mesh axis runs over, the one named last changes fastest.
Arguments:
- probes: bfloat16 [2, 16, 16384], P(None, None, ('region', 'blk')), may hold values from -6 to 6
- near_blocks: bfloat16 [3, 2, 16384, 512], P(None, None, ('region', 'blk')), may hold values from -0.078125 to 0.078125
- inner_basis: bfloat16 [2, 64, 16384], P(None, None, ('region', 'blk')), may hold values from -0.1875 to 0.1875
- coupling: bfloat16 [2, 2048, 512], P(None, ('region', 'blk')), may hold values from -0.1875 to 0.1875
- inner_expand: bfloat16 [2, 64, 16384], P(None, None, ('region', 'blk')), may hold values from -0.25 to 0.25
- outer_basis: bfloat16 [2, 256, 16384], P(None, None, ('region', 'blk')), may hold values from -0.1875 to 0.1875
- group_coupling: bfloat16 [2, 1024, 1024], P(None, 'region'), may hold values from -0.046875 to 0.046875
- outer_expand: bfloat16 [2, 256, 16384], P(None, None, ('region', 'blk')), may hold values from -0.125 to 0.125
- ranks: int32 [32], P(('region', 'blk')), may hold values from 8 to 64, as said below
Outputs:
- first: float32 [2, 16, 16384], P(None, None, ('region', 'blk'))
- second: float32 [2, 16, 16384], P(None, None, ('region', 'blk'))
The draws below stay inside these ranges and needn't reach their ends.
Inputs may be any that keep to these rules, and one draw needn't show every extreme that they name: `ranks`: some cluster has rank 64.
All inputs are finite; a program needn't handle non-finite values.
Results may differ from the reference program's by a relative error of at most 0.004.
Values may be sent and summed in bfloat16 or wider, within the bound.
A program may use at most 64 MiB of HBM per device.

```python
import jax
import jax.numpy as jnp
from jax import lax

NL = 512
P_SIZE = 16
R = 64
RG = 256
NTOT = 16384
N_REGION = 4
N_BLK = 8
DEVICES = 32


def draw_ranks(key, part):
    first_key, second_key = jax.random.split(jax.random.fold_in(key, 11))
    values = jax.random.randint(first_key, (DEVICES,), R // 8, R + 1)
    chosen = jax.random.randint(second_key, (), 0, DEVICES)
    return jnp.where(jnp.arange(DEVICES) == chosen, R, values).astype(jnp.int32)


def block_levels(key, shape, cuts, smallest, high):
    loudness, own = 1.0, jax.random.fold_in(key, 6)
    for dim, blocks in cuts:
        heights = jnp.exp(jax.random.uniform(jax.random.fold_in(own, dim), (blocks,), jnp.float32, smallest / len(cuts), high / len(cuts)))
        loudness = loudness * jnp.repeat(heights, shape[dim] // blocks).reshape([-1 if axis == dim else 1 for axis in range(len(shape))])
    return loudness


def centred(key, shape, width, limit, pieces=(), held_as=jnp.bfloat16):
    entries = jax.random.normal(key, shape, jnp.float32) * width
    if len(pieces) > 0:
        entries = block_levels(key, shape, pieces, -0.22, 0.18) * entries
    return jnp.clip(entries, min=-limit, max=limit).astype(held_as)


def setup_inputs(seed: int = 0) -> dict:
    key_of = jax.random.split(jax.random.key(seed), 10)
    return {
        "probes": centred(key_of[0], (2, P_SIZE, NTOT), 1.0, 6.0, ((2, 32),)),
        "near_blocks": centred(key_of[1], (3, 2, NTOT, NL), (10 * NL) ** -0.5, 0.078125, ((2, 32),)),
        "inner_basis": centred(key_of[2], (2, R, NTOT), (2 * NL) ** -0.5, 0.1875, ((2, 32),)),
        "coupling": centred(key_of[3], (2, R * DEVICES, N_BLK * R), (2 * R * N_BLK) ** -0.5, 0.1875, ((1, 32),)),
        "inner_expand": centred(key_of[4], (2, R, NTOT), (10 * R) ** -0.5, 0.25, ((2, 32),)),
        "outer_basis": centred(key_of[5], (2, RG, NTOT), (2 * NL) ** -0.5, 0.1875, ((2, 32),)),
        "group_coupling": centred(key_of[6], (2, N_REGION * RG, N_REGION * RG), (2 * RG * N_REGION * N_BLK) ** -0.5, 0.046875, ((1, 4),)),
        "outer_expand": centred(key_of[7], (2, RG, NTOT), (10 * RG) ** -0.5, 0.125, ((2, 32),)),
        "ranks": draw_ranks(jax.random.fold_in(key_of[9], 71), 0),
    }


def dots(vec, mat):
    return jnp.dot(vec, mat.T, preferred_element_type=jnp.float32)


def cmul(mat, vec):
    real = dots(vec[0], mat[0]) - dots(vec[1], mat[1])
    imag = dots(vec[1], mat[0]) + dots(vec[0], mat[1])
    return jnp.stack([real, imag])


def cexpand(vec, mat):
    real = jnp.dot(vec[0], mat[0], preferred_element_type=jnp.float32) - jnp.dot(vec[1], mat[1], preferred_element_type=jnp.float32)
    imag = jnp.dot(vec[1], mat[0], preferred_element_type=jnp.float32) + jnp.dot(vec[0], mat[1], preferred_element_type=jnp.float32)
    return jnp.stack([real, imag])


def cmul_high(mat, vec):
    high = lax.Precision.HIGHEST
    real = jnp.dot(vec[0], mat[0].T, precision=high) - jnp.dot(vec[1], mat[1].T, precision=high)
    imag = jnp.dot(vec[1], mat[0].T, precision=high) + jnp.dot(vec[0], mat[1].T, precision=high)
    return jnp.stack([real, imag])


def per_device(arr, rows):
    count = N_REGION * N_BLK
    return jnp.moveaxis(arr.reshape(arr.shape[0], rows, count, arr.shape[-1] // count), 2, 0)


def apply_operator(vec, near_blocks, inner_basis, coupling, inner_expand, outer_basis, group_coupling, outer_expand, ranks):
    count = N_REGION * N_BLK
    spans = jnp.moveaxis(vec.reshape(2, P_SIZE, count, NL), 2, 0)
    grouped = spans.reshape(N_REGION, N_BLK, 2, P_SIZE, NL)
    blank = jnp.zeros_like(grouped[:, :1])
    before = jnp.concatenate([blank, grouped[:, :-1]], 1).reshape(count, 2, P_SIZE, NL)
    after = jnp.concatenate([grouped[:, 1:], blank], 1).reshape(count, 2, P_SIZE, NL)
    near_dev = jnp.moveaxis(near_blocks.reshape(3, 2, count, NL, NL), 2, 0)
    inner_dev = per_device(inner_basis, R)
    outer_dev = per_device(outer_basis, RG)

    def local(item):
        blocks, left, centre, right, basis_in, basis_out = item
        near = cmul(blocks[0], left) + cmul(blocks[1], centre) + cmul(blocks[2], right)
        return near, cmul(basis_in, centre), cmul(basis_out, centre)

    near, coeff, wide = lax.map(local, (near_dev, before, spans, after, inner_dev, outer_dev))
    keep = jnp.arange(R, dtype=jnp.int32)[None, :] < ranks[:, None]
    coeff = jnp.where(keep[:, None, None, :], coeff, jnp.zeros_like(coeff)).astype(jnp.bfloat16)
    cgroups = coeff.reshape(N_REGION, N_BLK, 2, P_SIZE, R)
    coupling_dev = jnp.moveaxis(coupling.reshape(2, count, R, N_BLK * R), 1, 0)

    def inner_term(item):
        rows, index = item
        grp = lax.dynamic_index_in_dim(cgroups, index // N_BLK, 0, keepdims=False)
        distant = jnp.abs(jnp.arange(N_BLK, dtype=jnp.int32) - index % N_BLK) > 1
        grp = jnp.where(distant[:, None, None, None], grp, jnp.zeros_like(grp))
        stacked = jnp.transpose(grp, (1, 2, 0, 3)).reshape(2, P_SIZE, N_BLK * R)
        return cmul(rows, stacked).astype(jnp.bfloat16)

    inner = lax.map(inner_term, (coupling_dev, jnp.arange(count, dtype=jnp.int32)))
    gsum = jnp.sum(wide.reshape(N_REGION, N_BLK, 2, P_SIZE, RG), axis=1)
    gmats = jnp.moveaxis(group_coupling.reshape(2, N_REGION, RG, N_REGION * RG), 1, 0)

    def outer_term(item):
        rows, index = item
        others = jnp.arange(N_REGION, dtype=jnp.int32) != index
        masked = jnp.where(others[:, None, None, None], gsum, jnp.zeros_like(gsum))
        stacked = jnp.transpose(masked, (1, 2, 0, 3)).reshape(2, P_SIZE, N_REGION * RG)
        return cmul_high(rows.astype(gsum.dtype), stacked).astype(jnp.bfloat16)

    field = lax.map(outer_term, (gmats, jnp.arange(N_REGION, dtype=jnp.int32)))
    field_dev = jnp.repeat(field, N_BLK, axis=0)
    expand_in = per_device(inner_expand, R)
    expand_out = per_device(outer_expand, RG)

    def finish(item):
        near_part, inner_part, field_part, basis_in, basis_out = item
        return near_part + cexpand(inner_part, basis_in) + cexpand(field_part, basis_out)

    result = lax.map(finish, (near, inner, field_dev, expand_in, expand_out))
    return jnp.moveaxis(result, 0, 2).reshape(2, P_SIZE, count * NL)


def reference(probes, near_blocks, inner_basis, coupling, inner_expand, outer_basis, group_coupling, outer_expand, ranks):
    args = (near_blocks, inner_basis, coupling, inner_expand, outer_basis, group_coupling, outer_expand, ranks)
    first = apply_operator(probes, *args)
    second = apply_operator(first.astype(jnp.bfloat16), *args)
    return first, second
```

```python
import functools

import jax
import jax.numpy as jnp
from jax import lax
from jax.experimental import pallas as pl
from jax.experimental.pallas import tpu as pltpu
from jax.sharding import PartitionSpec as P

MESH = pl.DeviceIdType.MESH
F32 = jnp.float32
BF16 = jnp.bfloat16
TILE = 8
HALF = TILE // 2


def dot_t(vec, mat):
    return lax.dot_general(vec, mat, (((1,), (1,)), ((), ())), preferred_element_type=F32)


def dot(vec, mat):
    return jnp.dot(vec, mat, preferred_element_type=F32)


def times_i(x):
    rows, cols = x.shape
    x = x.reshape(rows // TILE, TILE, cols)
    turned = pltpu.roll(x, HALF, 1)
    upper = lax.broadcasted_iota(jnp.int32, x.shape, 1) < HALF
    return jnp.where(upper, -turned, turned).reshape(rows, cols)


def kernel(
    n_reg,
    n_blk,
    probes,
    near_blocks,
    inner_basis,
    coupling,
    inner_expand,
    outer_basis,
    group_coupling,
    outer_expand,
    ranks,
    first,
    second,
    v_in,
    nb,
    ib,
    cp,
    ie,
    ob,
    gc,
    oe,
    vbuf,
    nbr,
    wide_send,
    wide_recv,
    cbuf,
    fbuf,
    kmat,
    acc,
    load_sem,
    nbr_send,
    nbr_recv,
    wide_ssem,
    wide_rsem,
    c_ssem,
    c_rsem,
    f_ssem,
    f_rsem,
):
    region = lax.axis_index("region")
    pos = lax.axis_index("blk")
    rank_cap = ib.shape[1]
    group_rank = ob.shape[1]
    pages = wide_send.shape[1]
    stride = n_blk // pages
    slot = pos // stride
    reducer = lax.rem(pos, stride) == 0

    loads = [
        pltpu.make_async_copy(probes, v_in, load_sem.at[0]),
        pltpu.make_async_copy(outer_basis, ob, load_sem.at[1]),
        pltpu.make_async_copy(inner_basis, ib, load_sem.at[2]),
        pltpu.make_async_copy(near_blocks.at[1], nb.at[1], load_sem.at[3]),
        pltpu.make_async_copy(coupling, cp, load_sem.at[4]),
        pltpu.make_async_copy(group_coupling, gc, load_sem.at[5]),
        pltpu.make_async_copy(near_blocks.at[0], nb.at[0], load_sem.at[6]),
        pltpu.make_async_copy(near_blocks.at[2], nb.at[2], load_sem.at[7]),
        pltpu.make_async_copy(inner_expand, ie, load_sem.at[8]),
        pltpu.make_async_copy(outer_expand, oe, load_sem.at[9]),
    ]
    for load in loads:
        load.start()

    barrier = pltpu.get_barrier_semaphore()
    for off in range(1, n_blk):
        pl.semaphore_signal(
            barrier, inc=1, device_id=(region, lax.rem(pos + off, n_blk)), device_id_type=MESH
        )

    @pl.when(reducer)
    def _():
        for off in range(1, n_reg):
            for j in range(n_blk):
                pl.semaphore_signal(
                    barrier, inc=1, device_id=(lax.rem(region + off, n_reg), j), device_id_type=MESH
                )

    loads[0].wait()
    parts = [v_in[0].astype(F32), v_in[1].astype(F32)]
    start = jnp.concatenate(
        [parts[c][k * HALF : (k + 1) * HALF] for k in range(pages) for c in range(2)], axis=0
    )
    pl.semaphore_wait(barrier, n_blk - 1 + (n_reg - 1) * pages)

    def to_next(a):
        return pltpu.make_async_remote_copy(
            src_ref=vbuf.at[a],
            dst_ref=nbr.at[a, 0],
            send_sem=nbr_send.at[a, 0],
            recv_sem=nbr_recv.at[a, 0],
            device_id=(region, pos + 1),
            device_id_type=MESH,
        )

    def to_prev(a):
        return pltpu.make_async_remote_copy(
            src_ref=vbuf.at[a],
            dst_ref=nbr.at[a, 1],
            send_sem=nbr_send.at[a, 1],
            recv_sem=nbr_recv.at[a, 1],
            device_id=(region, pos - 1),
            device_id_type=MESH,
        )

    def wait_bytes(ref, sem):
        pltpu.make_async_copy(ref, ref, sem).wait()

    def apply(a, full):
        vec, ivec = full.astype(BF16), times_i(full).astype(BF16)
        vbuf[a] = vec

        @pl.when(pos < n_blk - 1)
        def _():
            to_next(a).start()

        @pl.when(pos > 0)
        def _():
            to_prev(a).start()

        if a == 0:
            loads[1].wait()
        wide = dot_t(vec, ob[0]) + dot_t(ivec, ob[1])
        wide_send[a] = wide.reshape(pages, TILE, group_rank)
        for off in range(1, n_reg):
            for k in range(pages):
                pltpu.make_async_remote_copy(
                    src_ref=wide_send.at[a, k],
                    dst_ref=wide_recv.at[a, off - 1, pos],
                    send_sem=wide_ssem.at[a],
                    recv_sem=wide_rsem.at[a],
                    device_id=(lax.rem(region + off, n_reg), k * stride),
                    device_id_type=MESH,
                ).start()

        if a == 0:
            loads[2].wait()
        coeff = dot_t(vec, ib[0]) + dot_t(ivec, ib[1])
        keep = lax.broadcasted_iota(jnp.int32, coeff.shape, 1) < ranks[0]
        coeff = jnp.where(keep, coeff, 0.0)
        cbuf[a, pos] = jnp.concatenate([coeff, times_i(coeff)], axis=1).astype(BF16)
        for off in range(1, n_blk):
            pltpu.make_async_remote_copy(
                src_ref=cbuf.at[a, pos],
                dst_ref=cbuf.at[a, pos],
                send_sem=c_ssem.at[a],
                recv_sem=c_rsem.at[a],
                device_id=(region, lax.rem(pos + off, n_blk)),
                device_id_type=MESH,
            ).start()

        if a == 0:
            loads[3].wait()
        acc[...] = dot_t(vec, nb[1, 0]) + dot_t(ivec, nb[1, 1])

        if a == 0:
            loads[4].wait()
            width = 2 * rank_cap
            lower = lax.broadcasted_iota(jnp.int32, (rank_cap, width), 1) < rank_cap
            for t in range(n_blk // 2):
                re = cp[0, :, t * width : (t + 1) * width].astype(F32)
                im = cp[1, :, t * width : (t + 1) * width].astype(F32)
                even = jnp.where(lower, re, pltpu.roll(im, rank_cap, 1))
                odd = jnp.where(lower, pltpu.roll(re, rank_cap, 1), im)
                for j, block in ((2 * t, even), (2 * t + 1, odd)):
                    far = (jnp.abs(pos - j) > 1).astype(F32)
                    kmat[:, j * width : (j + 1) * width] = (block * far).astype(BF16)
            loads[5].wait()

        @pl.when(reducer)
        def _():
            wait_bytes(wide_recv.at[a], wide_rsem.at[a])
            field = jnp.zeros((2 * TILE, group_rank), F32)
            for off in range(1, n_reg):
                total = wide_recv[a, off - 1, 0]
                for j in range(1, n_blk):
                    total = total + wide_recv[a, off - 1, j]
                high = total.astype(BF16).astype(F32)
                both = jnp.concatenate([high, total - high], axis=0)
                source = lax.rem(region - off + n_reg, n_reg)
                columns = pl.ds(pl.multiple_of(source * group_rank, group_rank), group_rank)
                field = field + dot_t(both.astype(BF16), gc[0, :, columns])
                field = field + dot_t(times_i(both).astype(BF16), gc[1, :, columns])
            fbuf[a, slot] = (field[:TILE] + field[TILE:]).astype(BF16).astype(F32)
            for off in range(1, n_blk):
                pltpu.make_async_remote_copy(
                    src_ref=fbuf.at[a, slot],
                    dst_ref=fbuf.at[a, slot],
                    send_sem=f_ssem.at[a],
                    recv_sem=f_rsem.at[a],
                    device_id=(region, lax.rem(pos + off, n_blk)),
                    device_id_type=MESH,
                ).start()

        if a == 0:
            loads[6].wait()
            loads[7].wait()

        @pl.when(pos > 0)
        def _():
            wait_bytes(nbr.at[a, 0], nbr_recv.at[a, 0])
            before = nbr[a, 0]
            turned = times_i(before.astype(F32)).astype(BF16)
            acc[...] += dot_t(before, nb[0, 0]) + dot_t(turned, nb[0, 1])

        @pl.when(pos < n_blk - 1)
        def _():
            wait_bytes(nbr.at[a, 1], nbr_recv.at[a, 1])
            after = nbr[a, 1]
            turned = times_i(after.astype(F32)).astype(BF16)
            acc[...] += dot_t(after, nb[2, 0]) + dot_t(turned, nb[2, 1])

        wait_bytes(cbuf.at[a, pl.ds(0, n_blk - 1)], c_rsem.at[a])
        piece = jnp.concatenate([cbuf[a, j] for j in range(n_blk)], axis=1)
        inner = dot_t(piece, kmat[...])
        if a == 0:
            loads[8].wait()
        acc[...] += dot(inner.astype(BF16), ie[0]) + dot(times_i(inner).astype(BF16), ie[1])

        if a == 0:
            loads[9].wait()

        @pl.when(reducer)
        def _():
            wait_bytes(fbuf.at[a, pl.ds(0, pages - 1)], f_rsem.at[a])

        @pl.when(jnp.logical_not(reducer))
        def _():
            wait_bytes(fbuf.at[a], f_rsem.at[a])

        field = fbuf[a].reshape(pages * TILE, group_rank)
        return acc[...] + dot(field.astype(BF16), oe[0]) + dot(times_i(field).astype(BF16), oe[1])

    def put(out, full):
        for k in range(pages):
            for c in range(2):
                lo = k * TILE + c * HALF
                out[c, k * HALF : (k + 1) * HALF, :] = full[lo : lo + HALF]

    one = apply(0, start)
    put(first, one)
    two = apply(1, one)
    put(second, two)

    for a in range(2):

        @pl.when(pos < n_blk - 1)
        def _():
            to_next(a).wait_send()

        @pl.when(pos > 0)
        def _():
            to_prev(a).wait_send()

        wait_bytes(wide_recv.at[a, :, pl.ds(0, pages)], wide_ssem.at[a])
        wait_bytes(cbuf.at[a, pl.ds(0, n_blk - 1)], c_ssem.at[a])

        @pl.when(reducer)
        def _():
            wait_bytes(wide_recv.at[a, 0, pl.ds(0, n_blk - 1)], f_ssem.at[a])


def solution(mesh):
    n_reg, n_blk = mesh.shape["region"], mesh.shape["blk"]
    both = ("region", "blk")

    def local(*args):
        probes, near_blocks, inner_basis, coupling, inner_expand = args[:5]
        outer_basis, group_coupling, outer_expand, _ = args[5:]
        _, vectors, width = probes.shape
        rows = 2 * vectors
        pages = rows // TILE
        rank_cap, group_rank = inner_basis.shape[1], outer_basis.shape[1]
        out = jax.ShapeDtypeStruct(probes.shape, F32)
        dma = pltpu.SemaphoreType.DMA
        return pl.pallas_call(
            functools.partial(kernel, n_reg, n_blk),
            out_shape=(out, out),
            in_specs=[pl.BlockSpec(memory_space=pl.ANY)] * 8
            + [pl.BlockSpec(memory_space=pltpu.SMEM)],
            out_specs=(pl.BlockSpec(memory_space=pltpu.VMEM),) * 2,
            scratch_shapes=[
                pltpu.VMEM(x.shape, BF16)
                for x in (
                    probes,
                    near_blocks,
                    inner_basis,
                    coupling,
                    inner_expand,
                    outer_basis,
                    group_coupling,
                    outer_expand,
                )
            ]
            + [
                pltpu.VMEM((2, rows, width), BF16),
                pltpu.VMEM((2, 2, rows, width), BF16),
                pltpu.VMEM((2, pages, TILE, group_rank), F32),
                pltpu.VMEM((2, n_reg - 1, n_blk, TILE, group_rank), F32),
                pltpu.VMEM((2, n_blk, rows, 2 * rank_cap), BF16),
                pltpu.VMEM((2, pages, TILE, group_rank), F32),
                pltpu.VMEM((rank_cap, n_blk * 2 * rank_cap), BF16),
                pltpu.VMEM((rows, width), F32),
                dma((10,)),
                dma((2, 2)),
                dma((2, 2)),
                dma((2,)),
                dma((2,)),
                dma((2,)),
                dma((2,)),
                dma((2,)),
                dma((2,)),
            ],
            compiler_params=pltpu.CompilerParams(
                collective_id=0, has_side_effects=True, vmem_limit_bytes=56 * 2**20
            ),
        )(*args)

    placed = (
        P(None, None, both),
        P(None, None, both, None),
        P(None, None, both),
        P(None, both, None),
        P(None, None, both),
        P(None, None, both),
        P(None, "region", None),
        P(None, None, both),
        P(both),
    )
    return jax.shard_map(
        local,
        mesh=mesh,
        in_specs=placed,
        out_specs=(P(None, None, both), P(None, None, both)),
        check_vma=False,
    )
```

```python
import functools

import jax
import jax.numpy as jnp
from jax import lax
from jax.experimental import pallas as pl
from jax.experimental.pallas import tpu as pltpu
from jax.sharding import PartitionSpec as P

MESH = pl.DeviceIdType.MESH
F32 = jnp.float32
BF16 = jnp.bfloat16
TILE = 16
HALF = TILE // 2


def dot_t(vec, mat):
    return lax.dot_general(vec, mat, (((1,), (1,)), ((), ())), preferred_element_type=F32)


def dot(vec, mat):
    return jnp.dot(vec, mat, preferred_element_type=F32)


def times_i(x):
    parts = []
    for lo in range(0, x.shape[0], TILE):
        parts += [-x[lo + HALF : lo + TILE], x[lo : lo + HALF]]
    return jnp.concatenate(parts, axis=0)


def kernel(
    n_reg,
    n_blk,
    probes,
    near_blocks,
    inner_basis,
    coupling,
    inner_expand,
    outer_basis,
    group_coupling,
    outer_expand,
    ranks,
    first_near,
    first_far,
    second_near,
    second_far,
    v_in,
    nb,
    ib,
    cp,
    ie,
    ob,
    gc,
    oe,
    vbuf,
    nbr,
    wide_send,
    wide_recv,
    cbuf,
    fbuf,
    kmat,
    emat,
    acc,
    load_sem,
    nbr_send,
    nbr_recv,
    wide_ssem,
    wide_rsem,
    c_ssem,
    c_rsem,
    f_ssem,
    f_rsem,
):
    region = lax.axis_index("region")
    pos = lax.axis_index("blk")
    rank_cap = ib.shape[1]
    group_rank = ob.shape[1]
    pages = wide_send.shape[1]
    places = [n_blk // 2 - pages + 2 * k for k in range(pages)]
    reducer = functools.reduce(jnp.logical_or, [pos == place for place in places])

    loads = [
        pltpu.make_async_copy(probes, v_in, load_sem.at[0]),
        pltpu.make_async_copy(outer_basis, ob, load_sem.at[1]),
        pltpu.make_async_copy(inner_basis, ib, load_sem.at[2]),
        pltpu.make_async_copy(near_blocks.at[1], nb.at[1], load_sem.at[3]),
        pltpu.make_async_copy(coupling, cp, load_sem.at[4]),
        pltpu.make_async_copy(group_coupling, gc, load_sem.at[5]),
        pltpu.make_async_copy(near_blocks.at[0], nb.at[0], load_sem.at[6]),
        pltpu.make_async_copy(near_blocks.at[2], nb.at[2], load_sem.at[7]),
        pltpu.make_async_copy(inner_expand, ie, load_sem.at[8]),
        pltpu.make_async_copy(outer_expand, oe, load_sem.at[9]),
    ]
    for load in loads:
        load.start()

    barrier = pltpu.get_barrier_semaphore()
    for off in range(1, n_blk):
        pl.semaphore_signal(
            barrier, inc=1, device_id=(region, lax.rem(pos + off, n_blk)), device_id_type=MESH
        )

    @pl.when(reducer)
    def _():
        for off in range(1, n_reg):
            for j in range(n_blk):
                pl.semaphore_signal(
                    barrier, inc=1, device_id=(lax.rem(region + off, n_reg), j), device_id_type=MESH
                )

    loads[0].wait()
    parts = [v_in[0].astype(F32), v_in[1].astype(F32)]
    start = jnp.concatenate(
        [parts[c][k * HALF : (k + 1) * HALF] for k in range(pages) for c in range(2)], axis=0
    )

    def to_next(a):
        return pltpu.make_async_remote_copy(
            src_ref=vbuf.at[a],
            dst_ref=nbr.at[a, 0],
            send_sem=nbr_send.at[a, 0],
            recv_sem=nbr_recv.at[a, 0],
            device_id=(region, pos + 1),
            device_id_type=MESH,
        )

    def to_prev(a):
        return pltpu.make_async_remote_copy(
            src_ref=vbuf.at[a],
            dst_ref=nbr.at[a, 1],
            send_sem=nbr_send.at[a, 1],
            recv_sem=nbr_recv.at[a, 1],
            device_id=(region, pos - 1),
            device_id_type=MESH,
        )

    def wait_bytes(ref, sem):
        pltpu.make_async_copy(ref, ref, sem).wait()

    def apply(a, full):
        vec, ivec = full.astype(BF16), times_i(full).astype(BF16)
        vbuf[a] = vec

        def send_vec():
            @pl.when(pos < n_blk - 1)
            def _():
                to_next(a).start()

            @pl.when(pos > 0)
            def _():
                to_prev(a).start()

        if a == 0:
            loads[1].wait()
        else:
            send_vec()
        wide = dot_t(vec, ob[0]) + dot_t(ivec, ob[1])
        wide_send[a] = wide.astype(BF16).reshape(pages, TILE, group_rank)
        if a == 0:
            pl.semaphore_wait(barrier, n_blk - 1 + (n_reg - 1) * pages)
        for off in range(1, n_reg):
            for k in range(pages):
                pltpu.make_async_remote_copy(
                    src_ref=wide_send.at[a, k],
                    dst_ref=wide_recv.at[a, off - 1, pos],
                    send_sem=wide_ssem.at[a],
                    recv_sem=wide_rsem.at[a],
                    device_id=(lax.rem(region + off, n_reg), places[k]),
                    device_id_type=MESH,
                ).start()

        if a == 0:
            send_vec()
            loads[2].wait()
        coeff = dot_t(vec, ib[0]) + dot_t(ivec, ib[1])
        keep = lax.broadcasted_iota(jnp.int32, coeff.shape, 1) < ranks[0]
        coeff = jnp.where(keep, coeff, 0.0)
        groups = range(0, pages * TILE, TILE)
        real = jnp.concatenate([coeff[lo : lo + HALF] for lo in groups], axis=0)
        imag = jnp.concatenate([coeff[lo + HALF : lo + TILE] for lo in groups], axis=0)
        cbuf[a, pos] = jnp.concatenate([real, imag], axis=1).astype(BF16)
        for off in range(1, n_blk):
            pltpu.make_async_remote_copy(
                src_ref=cbuf.at[a, pos],
                dst_ref=cbuf.at[a, pos],
                send_sem=c_ssem.at[a],
                recv_sem=c_rsem.at[a],
                device_id=(region, lax.rem(pos + off, n_blk)),
                device_id_type=MESH,
            ).start()

        if a == 0:
            loads[3].wait()
        acc[...] = dot_t(vec, nb[1, 0]) + dot_t(ivec, nb[1, 1])

        if a == 0:
            loads[5].wait()

        @pl.when(reducer)
        def _():
            wait_bytes(wide_recv.at[a], wide_rsem.at[a])
            field = jnp.zeros((2 * TILE, group_rank), F32)
            for off in range(1, n_reg):
                total = wide_recv[a, off - 1, 0].astype(F32)
                for j in range(1, n_blk):
                    total = total + wide_recv[a, off - 1, j].astype(F32)
                high = total.astype(BF16).astype(F32)
                both = jnp.concatenate([high, total - high], axis=0)
                source = lax.rem(region - off + n_reg, n_reg)
                columns = pl.ds(pl.multiple_of(source * group_rank, group_rank), group_rank)
                field = field + dot_t(both.astype(BF16), gc[0, :, columns])
                field = field + dot_t(times_i(both).astype(BF16), gc[1, :, columns])
            page = (field[:TILE] + field[TILE:]).astype(BF16)
            for k, place in enumerate(places):

                @pl.when(pos == place)
                def _():
                    fbuf[a, k] = page
                    for off in range(1, n_blk):
                        pltpu.make_async_remote_copy(
                            src_ref=fbuf.at[a, k],
                            dst_ref=fbuf.at[a, k],
                            send_sem=f_ssem.at[a],
                            recv_sem=f_rsem.at[a],
                            device_id=(region, (place + off) % n_blk),
                            device_id_type=MESH,
                        ).start()

        if a == 0:
            loads[6].wait()
            loads[7].wait()

        @pl.when(pos > 0)
        def _():
            wait_bytes(nbr.at[a, 0], nbr_recv.at[a, 0])
            before = nbr[a, 0]
            turned = times_i(before.astype(F32)).astype(BF16)
            acc[...] += dot_t(before, nb[0, 0]) + dot_t(turned, nb[0, 1])

        @pl.when(pos < n_blk - 1)
        def _():
            wait_bytes(nbr.at[a, 1], nbr_recv.at[a, 1])
            after = nbr[a, 1]
            turned = times_i(after.astype(F32)).astype(BF16)
            acc[...] += dot_t(after, nb[2, 0]) + dot_t(turned, nb[2, 1])

        if a == 0:
            loads[4].wait()
            pair = 2 * rank_cap
            lower = lax.broadcasted_iota(jnp.int32, (rank_cap, pair), 1) < rank_cap
            for t in range(n_blk // 2):
                re = cp[0, :, t * pair : (t + 1) * pair].astype(F32)
                im = cp[1, :, t * pair : (t + 1) * pair].astype(F32)
                re_turned = pltpu.roll(re, rank_cap, 1)
                im_turned = pltpu.roll(im, rank_cap, 1)
                for j, top, low in (
                    (2 * t, (re, -im_turned), (im, re_turned)),
                    (2 * t + 1, (re_turned, -im), (im_turned, re)),
                ):
                    far = (jnp.abs(pos - j) > 1).astype(F32)
                    at = slice(j * pair, (j + 1) * pair)
                    kmat[:rank_cap, at] = (jnp.where(lower, *top) * far).astype(BF16)
                    kmat[rank_cap:, at] = (jnp.where(lower, *low) * far).astype(BF16)
            loads[8].wait()
            width = ie.shape[2]
            emat[:rank_cap, :width] = ie[0]
            emat[rank_cap:, :width] = (-ie[1].astype(F32)).astype(BF16)
            emat[:rank_cap, width:] = ie[1]
            emat[rank_cap:, width:] = ie[0]

        wait_bytes(cbuf.at[a, pl.ds(0, n_blk - 1)], c_rsem.at[a])
        piece = jnp.concatenate([cbuf[a, j] for j in range(n_blk)], axis=1)
        inner = dot_t(piece, kmat[...]).astype(BF16)
        spread = dot(inner, emat[...])
        half = spread.shape[1] // 2
        acc[...] += jnp.concatenate(
            [
                spread[k * HALF : (k + 1) * HALF, c * half : (c + 1) * half]
                for k in range(pages)
                for c in range(2)
            ],
            axis=0,
        )

        if a == 0:
            loads[9].wait()

        @pl.when(reducer)
        def _():
            wait_bytes(fbuf.at[a, pl.ds(0, pages - 1)], f_rsem.at[a])

        @pl.when(jnp.logical_not(reducer))
        def _():
            wait_bytes(fbuf.at[a], f_rsem.at[a])

        field = fbuf[a].reshape(pages * TILE, group_rank)
        turned = times_i(field.astype(F32)).astype(BF16)
        return acc[...], dot(field, oe[0]) + dot(turned, oe[1])

    def put(out, full):
        for k in range(pages):
            for c in range(2):
                lo = k * TILE + c * HALF
                out[c, k * HALF : (k + 1) * HALF, :] = full[lo : lo + HALF]

    near, far = apply(0, start)
    put(first_near, near)
    put(first_far, far)
    near, far = apply(1, near + far)
    put(second_near, near)
    put(second_far, far)

    for a in range(2):

        @pl.when(pos < n_blk - 1)
        def _():
            to_next(a).wait_send()

        @pl.when(pos > 0)
        def _():
            to_prev(a).wait_send()

        wait_bytes(wide_recv.at[a, :, pl.ds(0, pages)], wide_ssem.at[a])
        wait_bytes(cbuf.at[a, pl.ds(0, n_blk - 1)], c_ssem.at[a])

        @pl.when(reducer)
        def _():
            wait_bytes(wide_recv.at[a, 0, pl.ds(0, n_blk - 1)], f_ssem.at[a])


def solution(mesh):
    n_reg, n_blk = mesh.shape["region"], mesh.shape["blk"]
    both = ("region", "blk")

    def local(*args):
        probes, near_blocks, inner_basis, coupling, inner_expand = args[:5]
        outer_basis, group_coupling, outer_expand, _ = args[5:]
        _, vectors, width = probes.shape
        rows = 2 * vectors
        pages = rows // TILE
        rank_cap, group_rank = inner_basis.shape[1], outer_basis.shape[1]
        out = jax.ShapeDtypeStruct(probes.shape, F32)
        dma = pltpu.SemaphoreType.DMA
        parts = pl.pallas_call(
            functools.partial(kernel, n_reg, n_blk),
            out_shape=(out,) * 4,
            in_specs=[pl.BlockSpec(memory_space=pl.ANY)] * 8
            + [pl.BlockSpec(memory_space=pltpu.SMEM)],
            out_specs=(pl.BlockSpec(memory_space=pltpu.VMEM),) * 4,
            scratch_shapes=[
                pltpu.VMEM(x.shape, BF16)
                for x in (
                    probes,
                    near_blocks,
                    inner_basis,
                    coupling,
                    inner_expand,
                    outer_basis,
                    group_coupling,
                    outer_expand,
                )
            ]
            + [
                pltpu.VMEM((2, rows, width), BF16),
                pltpu.VMEM((2, 2, rows, width), BF16),
                pltpu.VMEM((2, pages, TILE, group_rank), BF16),
                pltpu.VMEM((2, n_reg - 1, n_blk, TILE, group_rank), BF16),
                pltpu.VMEM((2, n_blk, vectors, 2 * rank_cap), BF16),
                pltpu.VMEM((2, pages, TILE, group_rank), BF16),
                pltpu.VMEM((2 * rank_cap, n_blk * 2 * rank_cap), BF16),
                pltpu.VMEM((2 * rank_cap, 2 * width), BF16),
                pltpu.VMEM((rows, width), F32),
                dma((10,)),
                dma((2, 2)),
                dma((2, 2)),
                dma((2,)),
                dma((2,)),
                dma((2,)),
                dma((2,)),
                dma((2,)),
                dma((2,)),
            ],
            compiler_params=pltpu.CompilerParams(
                collective_id=0, has_side_effects=True, vmem_limit_bytes=56 * 2**20
            ),
        )(*args)
        return parts[0] + parts[1], parts[2] + parts[3]

    placed = (
        P(None, None, both),
        P(None, None, both, None),
        P(None, None, both),
        P(None, both, None),
        P(None, None, both),
        P(None, None, both),
        P(None, "region", None),
        P(None, None, both),
        P(both),
    )
    return jax.shard_map(
        local,
        mesh=mesh,
        in_specs=placed,
        out_specs=(P(None, None, both), P(None, None, both)),
        check_vma=False,
    )
```

```python
import functools

import jax
import jax.numpy as jnp
from jax import lax
from jax.experimental import pallas as pl
from jax.experimental.pallas import tpu as pltpu
from jax.sharding import PartitionSpec as P

MESH = pl.DeviceIdType.MESH
F32 = jnp.float32
BF16 = jnp.bfloat16
TILE = 16
HALF = TILE // 2


def dot_t(vec, mat):
    return lax.dot_general(vec, mat, (((1,), (1,)), ((), ())), preferred_element_type=F32)


def dot(vec, mat):
    return jnp.dot(vec, mat, preferred_element_type=F32)


def times_i(x):
    parts = []
    for lo in range(0, x.shape[0], TILE):
        parts += [-x[lo + HALF : lo + TILE], x[lo : lo + HALF]]
    return jnp.concatenate(parts, axis=0)


def kernel(
    n_reg,
    n_blk,
    probes,
    near_blocks,
    inner_basis,
    coupling,
    inner_expand,
    outer_basis,
    group_coupling,
    outer_expand,
    ranks,
    first,
    second,
    v_in,
    nb,
    ib,
    cp,
    ie,
    ob,
    gc,
    oe,
    vbuf,
    nbr,
    wide_send,
    wide_recv,
    cbuf,
    fbuf,
    kmat,
    emat,
    acc,
    load_sem,
    nbr_send,
    nbr_recv,
    wide_ssem,
    wide_rsem,
    c_ssem,
    c_rsem,
    f_ssem,
    f_rsem,
):
    region = lax.axis_index("region")
    pos = lax.axis_index("blk")
    rank_cap = ib.shape[1]
    group_rank = ob.shape[1]
    pages = wide_send.shape[1]
    places = [n_blk // 2 - pages + 2 * k for k in range(pages)]
    reducer = functools.reduce(jnp.logical_or, [pos == place for place in places])

    loads = [
        pltpu.make_async_copy(probes, v_in, load_sem.at[0]),
        pltpu.make_async_copy(outer_basis, ob, load_sem.at[1]),
        pltpu.make_async_copy(inner_basis, ib, load_sem.at[2]),
        pltpu.make_async_copy(near_blocks.at[1], nb.at[1], load_sem.at[3]),
        pltpu.make_async_copy(coupling, cp, load_sem.at[4]),
        pltpu.make_async_copy(group_coupling, gc, load_sem.at[5]),
        pltpu.make_async_copy(near_blocks.at[0], nb.at[0], load_sem.at[6]),
        pltpu.make_async_copy(near_blocks.at[2], nb.at[2], load_sem.at[7]),
        pltpu.make_async_copy(inner_expand, ie, load_sem.at[8]),
        pltpu.make_async_copy(outer_expand, oe, load_sem.at[9]),
    ]
    loads[0].start()
    loads[1].start()

    barrier = pltpu.get_barrier_semaphore()
    for off in range(1, n_blk):
        pl.semaphore_signal(
            barrier, inc=1, device_id=(region, lax.rem(pos + off, n_blk)), device_id_type=MESH
        )

    @pl.when(reducer)
    def _():
        for off in range(1, n_reg):
            for j in range(n_blk):
                pl.semaphore_signal(
                    barrier, inc=1, device_id=(lax.rem(region + off, n_reg), j), device_id_type=MESH
                )

    for load in loads[2:]:
        load.start()
    loads[0].wait()
    parts = [v_in[0].astype(F32), v_in[1].astype(F32)]
    start = jnp.concatenate(
        [parts[c][k * HALF : (k + 1) * HALF] for k in range(pages) for c in range(2)], axis=0
    )

    def to_next(a):
        return pltpu.make_async_remote_copy(
            src_ref=vbuf.at[a],
            dst_ref=nbr.at[a, 0],
            send_sem=nbr_send.at[a, 0],
            recv_sem=nbr_recv.at[a, 0],
            device_id=(region, pos + 1),
            device_id_type=MESH,
        )

    def to_prev(a):
        return pltpu.make_async_remote_copy(
            src_ref=vbuf.at[a],
            dst_ref=nbr.at[a, 1],
            send_sem=nbr_send.at[a, 1],
            recv_sem=nbr_recv.at[a, 1],
            device_id=(region, pos - 1),
            device_id_type=MESH,
        )

    def wait_bytes(ref, sem):
        pltpu.make_async_copy(ref, ref, sem).wait()

    def apply(a, full):
        vec, ivec = full.astype(BF16), times_i(full).astype(BF16)
        vbuf[a] = vec

        def send_vec():
            @pl.when(pos < n_blk - 1)
            def _():
                to_next(a).start()

            @pl.when(pos > 0)
            def _():
                to_prev(a).start()

        if a == 0:
            loads[1].wait()
        wide = dot_t(vec, ob[0]) + dot_t(ivec, ob[1])
        wide_send[a] = wide.astype(BF16).reshape(pages, TILE, group_rank)
        if a == 0:
            pl.semaphore_wait(barrier, n_blk - 1 + (n_reg - 1) * pages)
        for off in range(1, n_reg):
            for k in range(pages):
                pltpu.make_async_remote_copy(
                    src_ref=wide_send.at[a, k],
                    dst_ref=wide_recv.at[a, off - 1, pos],
                    send_sem=wide_ssem.at[a],
                    recv_sem=wide_rsem.at[a, off - 1],
                    device_id=(lax.rem(region + off, n_reg), places[k]),
                    device_id_type=MESH,
                ).start()

        send_vec()
        if a == 0:
            loads[2].wait()
        coeff = dot_t(vec, ib[0]) + dot_t(ivec, ib[1])
        keep = lax.broadcasted_iota(jnp.int32, coeff.shape, 1) < ranks[0]
        coeff = jnp.where(keep, coeff, 0.0)
        groups = range(0, pages * TILE, TILE)
        real = jnp.concatenate([coeff[lo : lo + HALF] for lo in groups], axis=0)
        imag = jnp.concatenate([coeff[lo + HALF : lo + TILE] for lo in groups], axis=0)
        cbuf[a, pos] = jnp.concatenate([real, imag], axis=1).astype(BF16)
        for off in range(1, n_blk):
            pltpu.make_async_remote_copy(
                src_ref=cbuf.at[a, pos],
                dst_ref=cbuf.at[a, pos],
                send_sem=c_ssem.at[a],
                recv_sem=c_rsem.at[a],
                device_id=(region, lax.rem(pos + off, n_blk)),
                device_id_type=MESH,
            ).start()

        if a == 0:
            loads[3].wait()
        acc[...] = dot_t(vec, nb[1, 0]) + dot_t(ivec, nb[1, 1])

        if a == 0:
            loads[5].wait()

        @pl.when(reducer)
        def _():
            field = jnp.zeros((2 * TILE, group_rank), F32)
            for off in range(1, n_reg):
                wait_bytes(wide_recv.at[a, off - 1], wide_rsem.at[a, off - 1])
                total = wide_recv[a, off - 1, 0].astype(F32)
                for j in range(1, n_blk):
                    total = total + wide_recv[a, off - 1, j].astype(F32)
                high = total.astype(BF16).astype(F32)
                both = jnp.concatenate([high, total - high], axis=0)
                source = lax.rem(region - off + n_reg, n_reg)
                columns = pl.ds(pl.multiple_of(source * group_rank, group_rank), group_rank)
                field = field + dot_t(both.astype(BF16), gc[0, :, columns])
                field = field + dot_t(times_i(both).astype(BF16), gc[1, :, columns])
            page = (field[:TILE] + field[TILE:]).astype(BF16)
            for k, place in enumerate(places):

                @pl.when(pos == place)
                def _():
                    fbuf[a, k] = page
                    for off in range(1, n_blk):
                        pltpu.make_async_remote_copy(
                            src_ref=fbuf.at[a, k],
                            dst_ref=fbuf.at[a, k],
                            send_sem=f_ssem.at[a],
                            recv_sem=f_rsem.at[a],
                            device_id=(region, (place + off) % n_blk),
                            device_id_type=MESH,
                        ).start()

        if a == 0:
            loads[6].wait()
            loads[7].wait()

        @pl.when(pos > 0)
        def _():
            wait_bytes(nbr.at[a, 0], nbr_recv.at[a, 0])
            before = nbr[a, 0]
            turned = times_i(before.astype(F32)).astype(BF16)
            acc[...] += dot_t(before, nb[0, 0]) + dot_t(turned, nb[0, 1])

        @pl.when(pos < n_blk - 1)
        def _():
            wait_bytes(nbr.at[a, 1], nbr_recv.at[a, 1])
            after = nbr[a, 1]
            turned = times_i(after.astype(F32)).astype(BF16)
            acc[...] += dot_t(after, nb[2, 0]) + dot_t(turned, nb[2, 1])

        if a == 0:
            loads[4].wait()
            pair = 2 * rank_cap
            lower = lax.broadcasted_iota(jnp.int32, (rank_cap, pair), 1) < rank_cap
            for t in range(n_blk // 2):
                re = cp[0, :, t * pair : (t + 1) * pair].astype(F32)
                im = cp[1, :, t * pair : (t + 1) * pair].astype(F32)
                re_turned = pltpu.roll(re, rank_cap, 1)
                im_turned = pltpu.roll(im, rank_cap, 1)
                for j, top, low in (
                    (2 * t, (re, -im_turned), (im, re_turned)),
                    (2 * t + 1, (re_turned, -im), (im_turned, re)),
                ):
                    far = (jnp.abs(pos - j) > 1).astype(F32)
                    at = slice(j * pair, (j + 1) * pair)
                    kmat[:rank_cap, at] = (jnp.where(lower, *top) * far).astype(BF16)
                    kmat[rank_cap:, at] = (jnp.where(lower, *low) * far).astype(BF16)
            loads[8].wait()
            width = ie.shape[2]
            emat[:rank_cap, :width] = ie[0]
            emat[rank_cap:, :width] = (-ie[1].astype(F32)).astype(BF16)
            emat[:rank_cap, width:] = ie[1]
            emat[rank_cap:, width:] = ie[0]

        wait_bytes(cbuf.at[a, pl.ds(0, n_blk - 1)], c_rsem.at[a])
        piece = jnp.concatenate([cbuf[a, j] for j in range(n_blk)], axis=1)
        inner = dot_t(piece, kmat[...]).astype(BF16)
        spread = dot(inner, emat[...])
        half = spread.shape[1] // 2
        acc[...] += jnp.concatenate(
            [
                spread[k * HALF : (k + 1) * HALF, c * half : (c + 1) * half]
                for k in range(pages)
                for c in range(2)
            ],
            axis=0,
        )

        if a == 0:
            loads[9].wait()

        @pl.when(reducer)
        def _():
            wait_bytes(fbuf.at[a, pl.ds(0, pages - 1)], f_rsem.at[a])

        @pl.when(jnp.logical_not(reducer))
        def _():
            wait_bytes(fbuf.at[a], f_rsem.at[a])

        field = fbuf[a].reshape(pages * TILE, group_rank)
        turned = times_i(field.astype(F32)).astype(BF16)
        return acc[...] + (dot(field, oe[0]) + dot(turned, oe[1]))

    def put(out, full):
        for k in range(pages):
            for c in range(2):
                lo = k * TILE + c * HALF
                out[c, k * HALF : (k + 1) * HALF, :] = full[lo : lo + HALF]

    one = apply(0, start)
    put(first, one)
    put(second, apply(1, one))

    for a in range(2):

        @pl.when(pos < n_blk - 1)
        def _():
            to_next(a).wait_send()

        @pl.when(pos > 0)
        def _():
            to_prev(a).wait_send()

        wait_bytes(wide_recv.at[a, :, pl.ds(0, pages)], wide_ssem.at[a])
        wait_bytes(cbuf.at[a, pl.ds(0, n_blk - 1)], c_ssem.at[a])

        @pl.when(reducer)
        def _():
            wait_bytes(wide_recv.at[a, 0, pl.ds(0, n_blk - 1)], f_ssem.at[a])


def store(first, second, first_out, second_out, sem):
    copies = [
        pltpu.make_async_copy(first, first_out, sem.at[0]),
        pltpu.make_async_copy(second, second_out, sem.at[1]),
    ]
    for copy in copies:
        copy.start()
    for copy in copies:
        copy.wait()


def solution(mesh):
    n_reg, n_blk = mesh.shape["region"], mesh.shape["blk"]
    both = ("region", "blk")

    def local(*args):
        probes, near_blocks, inner_basis, coupling, inner_expand = args[:5]
        outer_basis, group_coupling, outer_expand, _ = args[5:]
        _, vectors, width = probes.shape
        rows = 2 * vectors
        pages = rows // TILE
        rank_cap, group_rank = inner_basis.shape[1], outer_basis.shape[1]
        out = pltpu.VMEM(probes.shape, F32)
        dma = pltpu.SemaphoreType.DMA
        parts = pl.pallas_call(
            functools.partial(kernel, n_reg, n_blk),
            out_shape=(out,) * 2,
            in_specs=[pl.BlockSpec(memory_space=pl.ANY)] * 8
            + [pl.BlockSpec(memory_space=pltpu.SMEM)],
            out_specs=(pl.BlockSpec(memory_space=pltpu.VMEM),) * 2,
            scratch_shapes=[
                pltpu.VMEM(x.shape, BF16)
                for x in (
                    probes,
                    near_blocks,
                    inner_basis,
                    coupling,
                    inner_expand,
                    outer_basis,
                    group_coupling,
                    outer_expand,
                )
            ]
            + [
                pltpu.VMEM((2, rows, width), BF16),
                pltpu.VMEM((2, 2, rows, width), BF16),
                pltpu.VMEM((2, pages, TILE, group_rank), BF16),
                pltpu.VMEM((2, n_reg - 1, n_blk, TILE, group_rank), BF16),
                pltpu.VMEM((2, n_blk, vectors, 2 * rank_cap), BF16),
                pltpu.VMEM((2, pages, TILE, group_rank), BF16),
                pltpu.VMEM((2 * rank_cap, n_blk * 2 * rank_cap), BF16),
                pltpu.VMEM((2 * rank_cap, 2 * width), BF16),
                pltpu.VMEM((rows, width), F32),
                dma((10,)),
                dma((2, 2)),
                dma((2, 2)),
                dma((2,)),
                dma((2, n_reg - 1)),
                dma((2,)),
                dma((2,)),
                dma((2,)),
                dma((2,)),
            ],
            compiler_params=pltpu.CompilerParams(
                collective_id=0, has_side_effects=True, vmem_limit_bytes=56 * 2**20
            ),
        )(*args)
        result = jax.ShapeDtypeStruct(probes.shape, F32)
        return pl.pallas_call(
            store,
            out_shape=(result, result),
            in_specs=[pl.BlockSpec(memory_space=pltpu.VMEM)] * 2,
            out_specs=(pl.BlockSpec(memory_space=pl.ANY),) * 2,
            scratch_shapes=[dma((2,))],
        )(*parts)

    placed = (
        P(None, None, both),
        P(None, None, both, None),
        P(None, None, both),
        P(None, both, None),
        P(None, None, both),
        P(None, None, both),
        P(None, "region", None),
        P(None, None, both),
        P(both),
    )
    return jax.shard_map(
        local,
        mesh=mesh,
        in_specs=placed,
        out_specs=(P(None, None, both), P(None, None, both)),
        check_vma=False,
    )
```

```python
import functools

import jax
import jax.numpy as jnp
from jax import lax
from jax.experimental import pallas as pl
from jax.experimental.pallas import tpu as pltpu
from jax.sharding import PartitionSpec as P

MESH = pl.DeviceIdType.MESH
F32 = jnp.float32
BF16 = jnp.bfloat16
TILE = 16
HALF = TILE // 2


def dot_t(vec, mat):
    return lax.dot_general(vec, mat, (((1,), (1,)), ((), ())), preferred_element_type=F32)


def dot(vec, mat):
    return jnp.dot(vec, mat, preferred_element_type=F32)


def times_i(x):
    parts = []
    for lo in range(0, x.shape[0], TILE):
        parts += [-x[lo + HALF : lo + TILE], x[lo : lo + HALF]]
    return jnp.concatenate(parts, axis=0)


def kernel(
    n_reg,
    n_blk,
    probes,
    near_blocks,
    inner_basis,
    coupling,
    inner_expand,
    outer_basis,
    group_coupling,
    outer_expand,
    ranks,
    first,
    second,
    v_in,
    nb,
    ib,
    cp,
    ie,
    ob,
    gc,
    oe,
    vbuf,
    nbr,
    wide_send,
    wide_recv,
    cbuf,
    fbuf,
    kmat,
    emat,
    acc,
    load_sem,
    nbr_send,
    nbr_recv,
    wide_ssem,
    wide_rsem,
    c_ssem,
    c_rsem,
    f_ssem,
    f_rsem,
):
    region = lax.axis_index("region")
    pos = lax.axis_index("blk")
    rank_cap = ib.shape[1]
    group_rank = ob.shape[1]
    pages = wide_send.shape[1]
    places = [n_blk // 2 - pages + 2 * k for k in range(pages)]
    reducer = functools.reduce(jnp.logical_or, [pos == place for place in places])

    loads = [
        pltpu.make_async_copy(probes, v_in, load_sem.at[0]),
        pltpu.make_async_copy(outer_basis, ob, load_sem.at[1]),
        pltpu.make_async_copy(inner_basis, ib, load_sem.at[2]),
        pltpu.make_async_copy(near_blocks.at[1], nb.at[1], load_sem.at[3]),
        pltpu.make_async_copy(coupling, cp, load_sem.at[4]),
        pltpu.make_async_copy(group_coupling, gc, load_sem.at[5]),
        pltpu.make_async_copy(near_blocks.at[0], nb.at[0], load_sem.at[6]),
        pltpu.make_async_copy(near_blocks.at[2], nb.at[2], load_sem.at[7]),
        pltpu.make_async_copy(inner_expand, ie, load_sem.at[8]),
        pltpu.make_async_copy(outer_expand, oe, load_sem.at[9]),
    ]
    loads[0].start()
    loads[1].start()

    barrier = pltpu.get_barrier_semaphore()
    for off in range(1, n_blk):
        pl.semaphore_signal(
            barrier, inc=1, device_id=(region, lax.rem(pos + off, n_blk)), device_id_type=MESH
        )

    @pl.when(reducer)
    def _():
        for off in range(1, n_reg):
            for j in range(n_blk):
                pl.semaphore_signal(
                    barrier, inc=1, device_id=(lax.rem(region + off, n_reg), j), device_id_type=MESH
                )

    for load in loads[2:]:
        load.start()
    loads[0].wait()
    parts = [v_in[0].astype(F32), v_in[1].astype(F32)]
    start = jnp.concatenate(
        [parts[c][k * HALF : (k + 1) * HALF] for k in range(pages) for c in range(2)], axis=0
    )

    def to_next(a):
        return pltpu.make_async_remote_copy(
            src_ref=vbuf.at[a],
            dst_ref=nbr.at[a, 0],
            send_sem=nbr_send.at[a, 0],
            recv_sem=nbr_recv.at[a, 0],
            device_id=(region, pos + 1),
            device_id_type=MESH,
        )

    def to_prev(a):
        return pltpu.make_async_remote_copy(
            src_ref=vbuf.at[a],
            dst_ref=nbr.at[a, 1],
            send_sem=nbr_send.at[a, 1],
            recv_sem=nbr_recv.at[a, 1],
            device_id=(region, pos - 1),
            device_id_type=MESH,
        )

    def wait_bytes(ref, sem):
        pltpu.make_async_copy(ref, ref, sem).wait()

    def apply(a, full):
        vec, ivec = full.astype(BF16), times_i(full).astype(BF16)
        vbuf[a] = vec

        def send_vec():
            @pl.when(pos < n_blk - 1)
            def _():
                to_next(a).start()

            @pl.when(pos > 0)
            def _():
                to_prev(a).start()

        if a == 0:
            loads[1].wait()
        wide = dot_t(vec, ob[0]) + dot_t(ivec, ob[1])
        wide_send[a] = wide.astype(BF16).reshape(pages, TILE, group_rank)
        if a == 0:
            pl.semaphore_wait(barrier, n_blk - 1 + (n_reg - 1) * pages)
        for off in range(1, n_reg):
            for k in range(pages):
                pltpu.make_async_remote_copy(
                    src_ref=wide_send.at[a, k],
                    dst_ref=wide_recv.at[a, off - 1, pos],
                    send_sem=wide_ssem.at[a],
                    recv_sem=wide_rsem.at[a, off - 1],
                    device_id=(lax.rem(region + off, n_reg), places[k]),
                    device_id_type=MESH,
                ).start()

        send_vec()
        if a == 0:
            loads[2].wait()
        coeff = dot_t(vec, ib[0]) + dot_t(ivec, ib[1])
        keep = lax.broadcasted_iota(jnp.int32, coeff.shape, 1) < ranks[0]
        coeff = jnp.where(keep, coeff, 0.0)
        groups = range(0, pages * TILE, TILE)
        real = jnp.concatenate([coeff[lo : lo + HALF] for lo in groups], axis=0)
        imag = jnp.concatenate([coeff[lo + HALF : lo + TILE] for lo in groups], axis=0)
        cbuf[a, pos] = jnp.concatenate([real, imag], axis=1).astype(BF16)
        for off in range(1, n_blk):
            pltpu.make_async_remote_copy(
                src_ref=cbuf.at[a, pos],
                dst_ref=cbuf.at[a, pos],
                send_sem=c_ssem.at[a],
                recv_sem=c_rsem.at[a],
                device_id=(region, lax.rem(pos + off, n_blk)),
                device_id_type=MESH,
            ).start()

        if a == 0:
            loads[3].wait()
        acc[...] = dot_t(vec, nb[1, 0]) + dot_t(ivec, nb[1, 1])

        if a == 0:
            loads[6].wait()

        @pl.when(pos > 0)
        def _():
            wait_bytes(nbr.at[a, 0], nbr_recv.at[a, 0])
            before = nbr[a, 0]
            turned = times_i(before.astype(F32)).astype(BF16)
            acc[...] += dot_t(before, nb[0, 0]) + dot_t(turned, nb[0, 1])

        if a == 0:
            loads[5].wait()

        @pl.when(reducer)
        def _():
            field = jnp.zeros((2 * TILE, group_rank), F32)
            for off in range(1, n_reg):
                wait_bytes(wide_recv.at[a, off - 1], wide_rsem.at[a, off - 1])
                total = wide_recv[a, off - 1, 0].astype(F32)
                for j in range(1, n_blk):
                    total = total + wide_recv[a, off - 1, j].astype(F32)
                high = total.astype(BF16).astype(F32)
                both = jnp.concatenate([high, total - high], axis=0)
                source = lax.rem(region - off + n_reg, n_reg)
                columns = pl.ds(pl.multiple_of(source * group_rank, group_rank), group_rank)
                field = field + dot_t(both.astype(BF16), gc[0, :, columns])
                field = field + dot_t(times_i(both).astype(BF16), gc[1, :, columns])
            page = (field[:TILE] + field[TILE:]).astype(BF16)
            for k, place in enumerate(places):

                @pl.when(pos == place)
                def _():
                    fbuf[a, k] = page
                    for off in range(1, n_blk):
                        pltpu.make_async_remote_copy(
                            src_ref=fbuf.at[a, k],
                            dst_ref=fbuf.at[a, k],
                            send_sem=f_ssem.at[a],
                            recv_sem=f_rsem.at[a],
                            device_id=(region, (place + off) % n_blk),
                            device_id_type=MESH,
                        ).start()

        if a == 0:
            loads[7].wait()

        @pl.when(pos < n_blk - 1)
        def _():
            wait_bytes(nbr.at[a, 1], nbr_recv.at[a, 1])
            after = nbr[a, 1]
            turned = times_i(after.astype(F32)).astype(BF16)
            acc[...] += dot_t(after, nb[2, 0]) + dot_t(turned, nb[2, 1])

        if a == 0:
            loads[4].wait()
            pair = 2 * rank_cap
            lower = lax.broadcasted_iota(jnp.int32, (rank_cap, pair), 1) < rank_cap
            for t in range(n_blk // 2):
                re = cp[0, :, t * pair : (t + 1) * pair].astype(F32)
                im = cp[1, :, t * pair : (t + 1) * pair].astype(F32)
                re_turned = pltpu.roll(re, rank_cap, 1)
                im_turned = pltpu.roll(im, rank_cap, 1)
                for j, top, low in (
                    (2 * t, (re, -im_turned), (im, re_turned)),
                    (2 * t + 1, (re_turned, -im), (im_turned, re)),
                ):
                    far = (jnp.abs(pos - j) > 1).astype(F32)
                    at = slice(j * pair, (j + 1) * pair)
                    kmat[:rank_cap, at] = (jnp.where(lower, *top) * far).astype(BF16)
                    kmat[rank_cap:, at] = (jnp.where(lower, *low) * far).astype(BF16)
            loads[8].wait()
            width = ie.shape[2]
            emat[:rank_cap, :width] = ie[0]
            emat[rank_cap:, :width] = (-ie[1].astype(F32)).astype(BF16)
            emat[:rank_cap, width:] = ie[1]
            emat[rank_cap:, width:] = ie[0]

        wait_bytes(cbuf.at[a, pl.ds(0, n_blk - 1)], c_rsem.at[a])
        piece = jnp.concatenate([cbuf[a, j] for j in range(n_blk)], axis=1)
        inner = dot_t(piece, kmat[...]).astype(BF16)
        spread = dot(inner, emat[...])
        half = spread.shape[1] // 2
        acc[...] += jnp.concatenate(
            [
                spread[k * HALF : (k + 1) * HALF, c * half : (c + 1) * half]
                for k in range(pages)
                for c in range(2)
            ],
            axis=0,
        )

        if a == 0:
            loads[9].wait()

        @pl.when(reducer)
        def _():
            wait_bytes(fbuf.at[a, pl.ds(0, pages - 1)], f_rsem.at[a])

        @pl.when(jnp.logical_not(reducer))
        def _():
            wait_bytes(fbuf.at[a], f_rsem.at[a])

        field = fbuf[a].reshape(pages * TILE, group_rank)
        turned = times_i(field.astype(F32)).astype(BF16)
        return acc[...] + (dot(field, oe[0]) + dot(turned, oe[1]))

    def put(out, full):
        for k in range(pages):
            for c in range(2):
                lo = k * TILE + c * HALF
                out[c, k * HALF : (k + 1) * HALF, :] = full[lo : lo + HALF]

    one = apply(0, start)
    put(first, one)
    put(second, apply(1, one))

    for a in range(2):

        @pl.when(pos < n_blk - 1)
        def _():
            to_next(a).wait_send()

        @pl.when(pos > 0)
        def _():
            to_prev(a).wait_send()

        wait_bytes(wide_recv.at[a, :, pl.ds(0, pages)], wide_ssem.at[a])
        wait_bytes(cbuf.at[a, pl.ds(0, n_blk - 1)], c_ssem.at[a])

        @pl.when(reducer)
        def _():
            wait_bytes(wide_recv.at[a, 0, pl.ds(0, n_blk - 1)], f_ssem.at[a])


def solution(mesh):
    n_reg, n_blk = mesh.shape["region"], mesh.shape["blk"]
    both = ("region", "blk")

    def local(*args):
        probes, near_blocks, inner_basis, coupling, inner_expand = args[:5]
        outer_basis, group_coupling, outer_expand, _ = args[5:]
        _, vectors, width = probes.shape
        rows = 2 * vectors
        pages = rows // TILE
        rank_cap, group_rank = inner_basis.shape[1], outer_basis.shape[1]
        out = pltpu.VMEM(probes.shape, F32)
        dma = pltpu.SemaphoreType.DMA
        return pl.pallas_call(
            functools.partial(kernel, n_reg, n_blk),
            out_shape=(out,) * 2,
            in_specs=[pl.BlockSpec(memory_space=pl.ANY)] * 8
            + [pl.BlockSpec(memory_space=pltpu.SMEM)],
            out_specs=(pl.BlockSpec(memory_space=pltpu.VMEM),) * 2,
            scratch_shapes=[
                pltpu.VMEM(x.shape, BF16)
                for x in (
                    probes,
                    near_blocks,
                    inner_basis,
                    coupling,
                    inner_expand,
                    outer_basis,
                    group_coupling,
                    outer_expand,
                )
            ]
            + [
                pltpu.VMEM((2, rows, width), BF16),
                pltpu.VMEM((2, 2, rows, width), BF16),
                pltpu.VMEM((2, pages, TILE, group_rank), BF16),
                pltpu.VMEM((2, n_reg - 1, n_blk, TILE, group_rank), BF16),
                pltpu.VMEM((2, n_blk, vectors, 2 * rank_cap), BF16),
                pltpu.VMEM((2, pages, TILE, group_rank), BF16),
                pltpu.VMEM((2 * rank_cap, n_blk * 2 * rank_cap), BF16),
                pltpu.VMEM((2 * rank_cap, 2 * width), BF16),
                pltpu.VMEM((rows, width), F32),
                dma((10,)),
                dma((2, 2)),
                dma((2, 2)),
                dma((2,)),
                dma((2, n_reg - 1)),
                dma((2,)),
                dma((2,)),
                dma((2,)),
                dma((2,)),
            ],
            compiler_params=pltpu.CompilerParams(
                collective_id=0, has_side_effects=True, vmem_limit_bytes=56 * 2**20
            ),
        )(*args)

    placed = (
        P(None, None, both),
        P(None, None, both, None),
        P(None, None, both),
        P(None, both, None),
        P(None, None, both),
        P(None, None, both),
        P(None, "region", None),
        P(None, None, both),
        P(both),
    )
    return jax.shard_map(
        local,
        mesh=mesh,
        in_specs=placed,
        out_specs=(P(None, None, both), P(None, None, both)),
        check_vma=False,
    )
```

```python
import functools

import jax
import jax.numpy as jnp
from jax import lax
from jax.experimental import pallas as pl
from jax.experimental.pallas import tpu as pltpu
from jax.sharding import PartitionSpec as P

MESH = pl.DeviceIdType.MESH
F32 = jnp.float32
BF16 = jnp.bfloat16
TILE = 16
HALF = TILE // 2


def dot_t(vec, mat):
    return lax.dot_general(vec, mat, (((1,), (1,)), ((), ())), preferred_element_type=F32)


def dot(vec, mat):
    return jnp.dot(vec, mat, preferred_element_type=F32)


def times_i(x):
    parts = []
    for lo in range(0, x.shape[0], TILE):
        parts += [-x[lo + HALF : lo + TILE], x[lo : lo + HALF]]
    return jnp.concatenate(parts, axis=0)


def kernel(
    n_reg,
    n_blk,
    probes,
    near_blocks,
    inner_basis,
    coupling,
    inner_expand,
    outer_basis,
    group_coupling,
    outer_expand,
    ranks,
    first,
    second,
    v_in,
    nb,
    ib,
    cp,
    ie,
    ob,
    gc,
    oe,
    vbuf,
    nbr,
    wide_send,
    wide_recv,
    sum_send,
    sum_recv,
    cbuf,
    fbuf,
    kmat,
    emat,
    acc,
    load_sem,
    nbr_send,
    nbr_recv,
    wide_ssem,
    wide_rsem,
    s_ssem,
    s_rsem,
    c_ssem,
    c_rsem,
    f_ssem,
    f_rsem,
):
    region = lax.axis_index("region")
    pos = lax.axis_index("blk")
    rank_cap = ib.shape[1]
    group_rank = ob.shape[1]
    pages = wide_send.shape[1]
    places = [n_blk // 2 - pages + 2 * k for k in range(pages)]
    reducer = functools.reduce(jnp.logical_or, [pos == place for place in places])

    loads = [
        pltpu.make_async_copy(probes, v_in, load_sem.at[0]),
        pltpu.make_async_copy(outer_basis, ob, load_sem.at[1]),
        pltpu.make_async_copy(inner_basis, ib, load_sem.at[2]),
        pltpu.make_async_copy(near_blocks.at[1], nb.at[1], load_sem.at[3]),
        pltpu.make_async_copy(coupling, cp, load_sem.at[4]),
        pltpu.make_async_copy(group_coupling, gc, load_sem.at[5]),
        pltpu.make_async_copy(near_blocks.at[0], nb.at[0], load_sem.at[6]),
        pltpu.make_async_copy(near_blocks.at[2], nb.at[2], load_sem.at[7]),
        pltpu.make_async_copy(inner_expand, ie, load_sem.at[8]),
        pltpu.make_async_copy(outer_expand, oe, load_sem.at[9]),
    ]
    loads[0].start()
    loads[1].start()

    barrier = pltpu.get_barrier_semaphore()
    for off in range(1, n_blk):
        pl.semaphore_signal(
            barrier, inc=1, device_id=(region, lax.rem(pos + off, n_blk)), device_id_type=MESH
        )

    @pl.when(reducer)
    def _():
        for off in range(1, n_reg):
            pl.semaphore_signal(
                barrier, inc=1, device_id=(lax.rem(region + off, n_reg), pos), device_id_type=MESH
            )

    for load in loads[2:]:
        load.start()
    loads[0].wait()
    parts = [v_in[0].astype(F32), v_in[1].astype(F32)]
    start = jnp.concatenate(
        [parts[c][k * HALF : (k + 1) * HALF] for k in range(pages) for c in range(2)], axis=0
    )

    def to_next(a):
        return pltpu.make_async_remote_copy(
            src_ref=vbuf.at[a],
            dst_ref=nbr.at[a, 0],
            send_sem=nbr_send.at[a, 0],
            recv_sem=nbr_recv.at[a, 0],
            device_id=(region, pos + 1),
            device_id_type=MESH,
        )

    def to_prev(a):
        return pltpu.make_async_remote_copy(
            src_ref=vbuf.at[a],
            dst_ref=nbr.at[a, 1],
            send_sem=nbr_send.at[a, 1],
            recv_sem=nbr_recv.at[a, 1],
            device_id=(region, pos - 1),
            device_id_type=MESH,
        )

    def wait_bytes(ref, sem):
        pltpu.make_async_copy(ref, ref, sem).wait()

    def apply(a, full):
        vec, ivec = full.astype(BF16), times_i(full).astype(BF16)
        vbuf[a] = vec

        def send_vec():
            @pl.when(pos < n_blk - 1)
            def _():
                to_next(a).start()

            @pl.when(pos > 0)
            def _():
                to_prev(a).start()

        if a == 0:
            loads[1].wait()
        wide = dot_t(vec, ob[0]) + dot_t(ivec, ob[1])
        wide = wide.astype(BF16).reshape(pages, TILE, group_rank)
        wide_send[a] = wide
        if a == 0:

            @pl.when(reducer)
            def _():
                pl.semaphore_wait(barrier, n_blk - 1 + n_reg - 1)

            @pl.when(jnp.logical_not(reducer))
            def _():
                pl.semaphore_wait(barrier, n_blk - 1)

        for k, place in enumerate(places):

            @pl.when(pos != place)
            def _():
                pltpu.make_async_remote_copy(
                    src_ref=wide_send.at[a, k],
                    dst_ref=wide_recv.at[a, pos],
                    send_sem=wide_ssem.at[a],
                    recv_sem=wide_rsem.at[a],
                    device_id=(region, place),
                    device_id_type=MESH,
                ).start()

            @pl.when(pos == place)
            def _():
                wide_recv[a, place] = wide[k]

        send_vec()
        if a == 0:
            loads[2].wait()
        coeff = dot_t(vec, ib[0]) + dot_t(ivec, ib[1])
        keep = lax.broadcasted_iota(jnp.int32, coeff.shape, 1) < ranks[0]
        coeff = jnp.where(keep, coeff, 0.0)
        groups = range(0, pages * TILE, TILE)
        real = jnp.concatenate([coeff[lo : lo + HALF] for lo in groups], axis=0)
        imag = jnp.concatenate([coeff[lo + HALF : lo + TILE] for lo in groups], axis=0)
        cbuf[a, pos] = jnp.concatenate([real, imag], axis=1).astype(BF16)
        for off in range(1, n_blk):
            pltpu.make_async_remote_copy(
                src_ref=cbuf.at[a, pos],
                dst_ref=cbuf.at[a, pos],
                send_sem=c_ssem.at[a],
                recv_sem=c_rsem.at[a],
                device_id=(region, lax.rem(pos + off, n_blk)),
                device_id_type=MESH,
            ).start()

        @pl.when(reducer)
        def _():
            wait_bytes(wide_recv.at[a, pl.ds(0, n_blk - 1)], wide_rsem.at[a])
            total = wide_recv[a, 0].astype(F32)
            for j in range(1, n_blk):
                total = total + wide_recv[a, j].astype(F32)
            sum_send[a] = total
            for off in range(1, n_reg):
                pltpu.make_async_remote_copy(
                    src_ref=sum_send.at[a],
                    dst_ref=sum_recv.at[a, off - 1],
                    send_sem=s_ssem.at[a],
                    recv_sem=s_rsem.at[a, off - 1],
                    device_id=(lax.rem(region + off, n_reg), pos),
                    device_id_type=MESH,
                ).start()

        if a == 0:
            loads[3].wait()
        acc[...] = dot_t(vec, nb[1, 0]) + dot_t(ivec, nb[1, 1])

        if a == 0:
            loads[6].wait()

        @pl.when(pos > 0)
        def _():
            wait_bytes(nbr.at[a, 0], nbr_recv.at[a, 0])
            before = nbr[a, 0]
            turned = times_i(before.astype(F32)).astype(BF16)
            acc[...] += dot_t(before, nb[0, 0]) + dot_t(turned, nb[0, 1])

        if a == 0:
            loads[5].wait()

        @pl.when(reducer)
        def _():
            field = jnp.zeros((2 * TILE, group_rank), F32)
            for off in range(1, n_reg):
                wait_bytes(sum_recv.at[a, off - 1], s_rsem.at[a, off - 1])
                total = sum_recv[a, off - 1]
                high = total.astype(BF16).astype(F32)
                both = jnp.concatenate([high, total - high], axis=0)
                source = lax.rem(region - off + n_reg, n_reg)
                columns = pl.ds(pl.multiple_of(source * group_rank, group_rank), group_rank)
                field = field + dot_t(both.astype(BF16), gc[0, :, columns])
                field = field + dot_t(times_i(both).astype(BF16), gc[1, :, columns])
            page = (field[:TILE] + field[TILE:]).astype(BF16)
            for k, place in enumerate(places):

                @pl.when(pos == place)
                def _():
                    fbuf[a, k] = page
                    for off in range(1, n_blk):
                        pltpu.make_async_remote_copy(
                            src_ref=fbuf.at[a, k],
                            dst_ref=fbuf.at[a, k],
                            send_sem=f_ssem.at[a],
                            recv_sem=f_rsem.at[a],
                            device_id=(region, (place + off) % n_blk),
                            device_id_type=MESH,
                        ).start()

        if a == 0:
            loads[7].wait()

        @pl.when(pos < n_blk - 1)
        def _():
            wait_bytes(nbr.at[a, 1], nbr_recv.at[a, 1])
            after = nbr[a, 1]
            turned = times_i(after.astype(F32)).astype(BF16)
            acc[...] += dot_t(after, nb[2, 0]) + dot_t(turned, nb[2, 1])

        if a == 0:
            loads[4].wait()
            pair = 2 * rank_cap
            lower = lax.broadcasted_iota(jnp.int32, (rank_cap, pair), 1) < rank_cap
            for t in range(n_blk // 2):
                re = cp[0, :, t * pair : (t + 1) * pair].astype(F32)
                im = cp[1, :, t * pair : (t + 1) * pair].astype(F32)
                re_turned = pltpu.roll(re, rank_cap, 1)
                im_turned = pltpu.roll(im, rank_cap, 1)
                for j, top, low in (
                    (2 * t, (re, -im_turned), (im, re_turned)),
                    (2 * t + 1, (re_turned, -im), (im_turned, re)),
                ):
                    far = (jnp.abs(pos - j) > 1).astype(F32)
                    at = slice(j * pair, (j + 1) * pair)
                    kmat[:rank_cap, at] = (jnp.where(lower, *top) * far).astype(BF16)
                    kmat[rank_cap:, at] = (jnp.where(lower, *low) * far).astype(BF16)
            loads[8].wait()
            width = ie.shape[2]
            emat[:rank_cap, :width] = ie[0]
            emat[rank_cap:, :width] = (-ie[1].astype(F32)).astype(BF16)
            emat[:rank_cap, width:] = ie[1]
            emat[rank_cap:, width:] = ie[0]

        wait_bytes(cbuf.at[a, pl.ds(0, n_blk - 1)], c_rsem.at[a])
        piece = jnp.concatenate([cbuf[a, j] for j in range(n_blk)], axis=1)
        inner = dot_t(piece, kmat[...]).astype(BF16)
        spread = dot(inner, emat[...])
        half = spread.shape[1] // 2
        acc[...] += jnp.concatenate(
            [
                spread[k * HALF : (k + 1) * HALF, c * half : (c + 1) * half]
                for k in range(pages)
                for c in range(2)
            ],
            axis=0,
        )

        if a == 0:
            loads[9].wait()

        @pl.when(reducer)
        def _():
            wait_bytes(fbuf.at[a, pl.ds(0, pages - 1)], f_rsem.at[a])

        @pl.when(jnp.logical_not(reducer))
        def _():
            wait_bytes(fbuf.at[a], f_rsem.at[a])

        field = fbuf[a].reshape(pages * TILE, group_rank)
        turned = times_i(field.astype(F32)).astype(BF16)
        return acc[...] + (dot(field, oe[0]) + dot(turned, oe[1]))

    def put(out, full):
        for k in range(pages):
            for c in range(2):
                lo = k * TILE + c * HALF
                out[c, k * HALF : (k + 1) * HALF, :] = full[lo : lo + HALF]

    one = apply(0, start)
    put(first, one)
    put(second, apply(1, one))

    for a in range(2):

        @pl.when(pos < n_blk - 1)
        def _():
            to_next(a).wait_send()

        @pl.when(pos > 0)
        def _():
            to_prev(a).wait_send()

        wait_bytes(cbuf.at[a, pl.ds(0, n_blk - 1)], c_ssem.at[a])

        @pl.when(reducer)
        def _():
            wait_bytes(wide_send.at[a, pl.ds(0, pages - 1)], wide_ssem.at[a])
            wait_bytes(sum_recv.at[a], s_ssem.at[a])
            wait_bytes(wide_recv.at[a, pl.ds(0, n_blk - 1)], f_ssem.at[a])

        @pl.when(jnp.logical_not(reducer))
        def _():
            wait_bytes(wide_send.at[a], wide_ssem.at[a])


def solution(mesh):
    n_reg, n_blk = mesh.shape["region"], mesh.shape["blk"]
    both = ("region", "blk")

    def local(*args):
        probes, near_blocks, inner_basis, coupling, inner_expand = args[:5]
        outer_basis, group_coupling, outer_expand, _ = args[5:]
        _, vectors, width = probes.shape
        rows = 2 * vectors
        pages = rows // TILE
        rank_cap, group_rank = inner_basis.shape[1], outer_basis.shape[1]
        out = pltpu.VMEM(probes.shape, F32)
        dma = pltpu.SemaphoreType.DMA
        return pl.pallas_call(
            functools.partial(kernel, n_reg, n_blk),
            out_shape=(out,) * 2,
            in_specs=[pl.BlockSpec(memory_space=pl.ANY)] * 8
            + [pl.BlockSpec(memory_space=pltpu.SMEM)],
            out_specs=(pl.BlockSpec(memory_space=pltpu.VMEM),) * 2,
            scratch_shapes=[
                pltpu.VMEM(x.shape, BF16)
                for x in (
                    probes,
                    near_blocks,
                    inner_basis,
                    coupling,
                    inner_expand,
                    outer_basis,
                    group_coupling,
                    outer_expand,
                )
            ]
            + [
                pltpu.VMEM((2, rows, width), BF16),
                pltpu.VMEM((2, 2, rows, width), BF16),
                pltpu.VMEM((2, pages, TILE, group_rank), BF16),
                pltpu.VMEM((2, n_blk, TILE, group_rank), BF16),
                pltpu.VMEM((2, TILE, group_rank), F32),
                pltpu.VMEM((2, n_reg - 1, TILE, group_rank), F32),
                pltpu.VMEM((2, n_blk, vectors, 2 * rank_cap), BF16),
                pltpu.VMEM((2, pages, TILE, group_rank), BF16),
                pltpu.VMEM((2 * rank_cap, n_blk * 2 * rank_cap), BF16),
                pltpu.VMEM((2 * rank_cap, 2 * width), BF16),
                pltpu.VMEM((rows, width), F32),
                dma((10,)),
                dma((2, 2)),
                dma((2, 2)),
                dma((2,)),
                dma((2,)),
                dma((2,)),
                dma((2, n_reg - 1)),
                dma((2,)),
                dma((2,)),
                dma((2,)),
                dma((2,)),
            ],
            compiler_params=pltpu.CompilerParams(
                collective_id=0, has_side_effects=True, vmem_limit_bytes=56 * 2**20
            ),
        )(*args)

    placed = (
        P(None, None, both),
        P(None, None, both, None),
        P(None, None, both),
        P(None, both, None),
        P(None, None, both),
        P(None, None, both),
        P(None, "region", None),
        P(None, None, both),
        P(both),
    )
    return jax.shard_map(
        local,
        mesh=mesh,
        in_specs=placed,
        out_specs=(P(None, None, both), P(None, None, both)),
        check_vma=False,
    )
```
